32 devices in a mesh: grid: 8 (over z, x), ch: 4 (over y, core).
Axes of the slice: x: 2, y: 2, z: 4, core: 2. Of those that a mesh axis runs over, the one named last changes fastest.
Arguments:
- inputs: bfloat16 [32, 1024, 512], P('grid', None, 'ch'), may hold values from -6 to 6
- w_gate: bfloat16 [512, 512], P(None, 'ch'), may hold values from -0.25 to 0.25
- w_value: bfloat16 [512, 512], P(None, 'ch'), may hold values from -0.25 to 0.25
- short_filter: bfloat16 [2, 3, 3, 512], P(None, None, None, 'ch'), may hold values from -2 to 2
- row_filter: bfloat16 [1024, 512], P(None, 'ch'), may hold values from -0.1875 to 0.1875
- column_filter: bfloat16 [32, 512], P(None, 'ch'), may hold values from -1 to 1
- cotangent: bfloat16 [32, 1024, 512], P('grid', None, 'ch'), may hold values from -6 to 6
Outputs:
- gated: bfloat16 [32, 1024, 512], P('grid', None, 'ch')
- input_grad: bfloat16 [32, 1024, 512], P('grid', None, 'ch')
- gate_grad: float32 [512, 512], P('grid', 'ch')
- value_grad: float32 [512, 512], P('grid', 'ch')
- short_grad: float32 [2, 3, 3, 512], P(None, None, None, 'ch')
- row_grad: float32 [1024, 512], P('grid', 'ch')
- column_grad: float32 [32, 512], P('grid', 'ch')
The draws below stay inside these ranges and needn't reach their ends.
All inputs are finite; a program needn't handle non-finite values.
Results may differ from the reference program's by a relative error of at most 0.025.
Values may be sent and summed in bfloat16 or wider, within the bound.
A program may use at most 128 MiB of HBM per device.

```python
import math
import jax
import jax.numpy as jnp
from jax import lax

D = 512
W = 1024
H = 32


def level_of(own_key, shape, pieces, low, largest):
    loudness, own = 1.0, jax.random.fold_in(own_key, 6)
    for position, blocks in pieces:
        draws = jnp.exp(jax.random.uniform(jax.random.fold_in(own, position), (blocks,), jnp.float32, low / len(pieces), largest / len(pieces)))
        loudness = loudness * jnp.repeat(draws, shape[position] // blocks).reshape([-1 if axis == position else 1 for axis in range(len(shape))])
    return loudness


def noise(own_key, shape, width, bound, cuts=(), dtype=jnp.bfloat16):
    entries = jax.random.normal(own_key, shape, jnp.float32) * width
    if len(cuts) > 0:
        entries = level_of(own_key, shape, cuts, -0.22, 0.18) * entries
    return jnp.clip(entries, min=-bound, max=bound).astype(dtype)


def setup_inputs(seed: int = 0) -> dict:
    splits = jax.random.split(jax.random.key(seed), 8)
    return {
        "inputs": noise(splits[0], (H, W, D), 1.0, 6.0, ((0, 8), (2, 4))),
        "w_gate": noise(splits[1], (D, D), D ** -0.5, 0.25, ((1, 4),)),
        "w_value": noise(splits[2], (D, D), D ** -0.5, 0.25, ((1, 4),)),
        "short_filter": noise(splits[3], (2, 3, 3, D), 9 ** -0.5, 2.0, ((3, 4),)),
        "row_filter": noise(splits[4], (W, D), W ** -0.5, 0.1875, ((1, 4),)),
        "column_filter": noise(splits[5], (H, D), H ** -0.5, 1.0, ((1, 4),)),
        "cotangent": noise(splits[6], (H, W, D), 1.0, 6.0, ((0, 8), (2, 4))),
    }


def featurize(field, kernel):
    height, breadth = (field.shape[0], field.shape[1])
    padded = jnp.pad(field, ((1, 1), (1, 1), (0, 0)))
    total = jnp.zeros_like(field)
    for row_shift in range(3):
        for col_shift in range(3):
            total = total + kernel[row_shift, col_shift] * padded[row_shift:row_shift + height, col_shift:col_shift + breadth]
    return total

def featurize_back(field, kernel):
    height, breadth = (field.shape[0], field.shape[1])
    padded = jnp.pad(field, ((1, 1), (1, 1), (0, 0)))
    total = jnp.zeros_like(field)
    for row_shift in range(3):
        for col_shift in range(3):
            total = total + kernel[row_shift, col_shift] * padded[2 - row_shift:2 - row_shift + height, 2 - col_shift:2 - col_shift + breadth]
    return total

def filter_terms(grad_field, source):
    height, breadth = (grad_field.shape[0], grad_field.shape[1])
    padded = jnp.pad(source, ((1, 1), (1, 1), (0, 0)))
    outer = []
    for row_shift in range(3):
        inner = []
        for col_shift in range(3):
            inner.append(lax.optimization_barrier(jnp.sum(grad_field * padded[row_shift:row_shift + height, col_shift:col_shift + breadth], axis=(0, 1))))
        outer.append(jnp.stack(inner))
    return jnp.stack(outer)

def reference(inputs, w_gate, w_value, short_filter, row_filter, column_filter, cotangent):
    height, breadth, depth = inputs.shape
    scale = 1.0 / math.sqrt(height * breadth)
    flat = inputs.reshape(height * breadth, depth)
    proj_a = jnp.dot(flat, w_gate, preferred_element_type=jnp.float32).astype(jnp.bfloat16).reshape(height, breadth, depth)
    proj_b = jnp.dot(flat, w_value, preferred_element_type=jnp.float32).astype(jnp.bfloat16).reshape(height, breadth, depth)
    kernel = short_filter.astype(jnp.float32)
    pa32 = proj_a.astype(jnp.float32)
    pb32 = proj_b.astype(jnp.float32)
    feat_a = featurize(pa32, kernel[0]).astype(jnp.bfloat16)
    feat_b = featurize(pb32, kernel[1]).astype(jnp.bfloat16)
    fa32 = feat_a.astype(jnp.float32)
    fb32 = feat_b.astype(jnp.float32)
    row_spec = jnp.fft.rfft(row_filter.astype(jnp.float32), axis=0)
    col_spec = jnp.fft.rfft(column_filter.astype(jnp.float32), axis=0)
    spec_b = jnp.fft.rfft(fb32, axis=1)
    mix_row = jnp.fft.irfft(spec_b * row_spec[None], n=breadth, axis=1)
    spec_row = jnp.fft.rfft(mix_row, axis=0)
    mix_col = jnp.fft.irfft(spec_row * col_spec[:, None], n=height, axis=0)
    gated = (fa32 * mix_col).astype(jnp.bfloat16)
    grad_out = cotangent.astype(jnp.float32)
    grad_a = grad_out * mix_col
    grad_col = grad_out * fa32
    spec_gc = jnp.fft.rfft(grad_col, axis=0)
    grad_row = jnp.fft.irfft(spec_gc * jnp.conj(col_spec)[:, None], n=height, axis=0)
    column_grad = jnp.fft.irfft(lax.optimization_barrier(jnp.sum(spec_gc * jnp.conj(spec_row), axis=1)), n=height, axis=0) * scale
    spec_gr = jnp.fft.rfft(grad_row, axis=1)
    grad_b = jnp.fft.irfft(spec_gr * jnp.conj(row_spec)[None], n=breadth, axis=1)
    row_grad = jnp.fft.irfft(lax.optimization_barrier(jnp.sum(spec_gr * jnp.conj(spec_b), axis=0)), n=breadth, axis=0) * scale
    back_a = featurize_back(grad_a, kernel[0]).astype(jnp.bfloat16)
    back_b = featurize_back(grad_b, kernel[1]).astype(jnp.bfloat16)
    short_grad = jnp.stack([filter_terms(grad_a, pa32), filter_terms(grad_b, pb32)]) * scale
    flat_a = back_a.reshape(height * breadth, depth)
    flat_b = back_b.reshape(height * breadth, depth)
    summed = jnp.dot(flat_a, w_gate.T, preferred_element_type=jnp.float32) + jnp.dot(flat_b, w_value.T, preferred_element_type=jnp.float32)
    input_grad = summed.astype(jnp.bfloat16).reshape(height, breadth, depth)
    gate_grad = jnp.dot(flat.T, flat_a, preferred_element_type=jnp.float32) * scale
    value_grad = jnp.dot(flat.T, flat_b, preferred_element_type=jnp.float32) * scale
    return (gated, input_grad, gate_grad, value_grad, short_grad.astype(jnp.float32), row_grad.astype(jnp.float32), column_grad.astype(jnp.float32))
```

```python
import math

import jax
import jax.numpy as jnp
import ml_dtypes
import numpy as np
from jax import lax
from jax.sharding import PartitionSpec as P

bf16 = jnp.bfloat16
f32 = jnp.float32


def basis(length, tiles):
    half = length // 2
    per = half // tiles
    position = np.arange(length)
    columns, weights = [], []
    for tile in range(tiles):
        freqs = np.arange(tile * per, (tile + 1) * per)
        phase = (position[:, None] * freqs[None, :] % length) * (2.0 * math.pi / length)
        sines = np.sin(phase)
        weight = np.full((2 * per,), 2.0 / length)
        if tile == 0:
            sines[:, 0] = np.where(position % 2 == 0, 1.0, -1.0)
            weight[0] = weight[per] = 1.0 / length
        columns += [np.cos(phase), sines]
        weights.append(weight)
    return np.concatenate(columns, axis=1), np.concatenate(weights)


def parts(spectrum, axis):
    return jnp.split(spectrum, 2, axis=axis)


def filter_parts(spectrum, first):
    cos, sin = parts(spectrum, 0)
    row = lax.broadcasted_iota(jnp.int32, cos.shape, 0) == 0
    packed = jnp.logical_and(row, first)
    return cos, jnp.where(packed, 0.0, sin), jnp.where(packed, sin, cos)


def times(spectrum, coef, axis):
    x, y = parts(spectrum, axis)
    p, q, p2 = coef
    return jnp.concatenate([x * p - y * q, x * q + y * p2], axis=axis)


def times_conj(spectrum, coef, axis):
    x, y = parts(spectrum, axis)
    p, q, p2 = coef
    return jnp.concatenate([x * p + y * q, y * p2 - x * q], axis=axis)


def correlate(a, b, axis, total, first):
    ax, ay = parts(a, axis)
    bx, by = parts(b, axis)
    xx, yy = jnp.sum(ax * bx, axis=total), jnp.sum(ay * by, axis=total)
    cross = jnp.sum(ay * bx - ax * by, axis=total)
    row = lax.broadcasted_iota(jnp.int32, xx.shape, 0) == 0
    packed = jnp.logical_and(row, first)
    return jnp.concatenate(
        [jnp.where(packed, xx, xx + yy), jnp.where(packed, yy, cross)], axis=0
    )


def dot(spec, a, b):
    return jnp.einsum(spec, a.astype(bf16), b.astype(bf16), preferred_element_type=f32)


def halo(value):
    size = lax.axis_size("grid")
    up = [(i, i + 1) for i in range(size - 1)]
    down = [(i + 1, i) for i in range(size - 1)]
    before = lax.ppermute(value[-1:], "grid", up)
    after = lax.ppermute(value[:1], "grid", down)
    return jnp.concatenate([before, value, after], axis=0)


def local(inputs, w_gate, w_value, short_filter, row_filter, column_filter, cotangent):
    tile_rows, width, channels = inputs.shape
    height = column_filter.shape[0]
    tiles = lax.axis_size("grid")
    me = lax.axis_index("grid")
    first = me == 0
    per = width // tiles
    scale = 1.0 / math.sqrt(height * width)

    wide, wide_weight = basis(width, tiles)
    tall, tall_weight = basis(height, 1)
    wide = jnp.asarray(wide.astype(ml_dtypes.bfloat16))
    tall = jnp.asarray(tall.astype(ml_dtypes.bfloat16))
    tall_weight = jnp.asarray(tall_weight, f32)[:, None]
    wide_weight = lax.dynamic_slice_in_dim(jnp.asarray(wide_weight, f32), me * per, per, 0)[:, None]
    wide_own = lax.dynamic_slice_in_dim(wide, me * per, per, 1)

    gathered = lax.all_gather(inputs, "ch", axis=2, tiled=True)
    w_both = jnp.concatenate([w_gate, w_value], axis=1)
    kernel = jnp.concatenate([short_filter[0], short_filter[1]], axis=-1).astype(f32)
    row_coef = filter_parts(dot("mk,mc->kc", wide_own, row_filter), first)
    col_coef = filter_parts(dot("mk,mc->kc", tall, column_filter), True)
    col_coef = tuple(v[:, None, :] for v in col_coef)

    stacked = dot("rwd,dc->rwc", gathered, w_both).astype(bf16)
    framed = jnp.pad(halo(stacked), ((0, 0), (1, 1), (0, 0)))
    featured = jnp.zeros((tile_rows, width, 2 * channels), f32)
    for i in range(3):
        for j in range(3):
            featured = featured + kernel[i, j] * framed[i : i + tile_rows, j : j + width].astype(f32)
    featured = featured.astype(bf16)
    gate_feat = featured[..., :channels].astype(f32)
    value_bf = featured[..., channels:]
    grad_out = cotangent.astype(f32)
    grad_mix = (grad_out * gate_feat).astype(bf16)

    def to_columns(field):
        spectrum = dot("wk,rwc->rkc", wide, field).astype(bf16)
        return lax.all_to_all(spectrum, "grid", split_axis=1, concat_axis=0, tiled=True).astype(f32)

    def to_rows(spectrum):
        spectrum = (spectrum * wide_weight).astype(bf16)
        back = lax.all_to_all(spectrum, "grid", split_axis=0, concat_axis=1, tiled=True)
        return dot("wk,rkc->rwc", wide, back)

    value_spec = to_columns(value_bf)
    grad_spec = to_columns(grad_mix)

    mixed_rows = times(value_spec, row_coef, 1)
    value_tall = dot("hk,hwc->kwc", tall, mixed_rows)
    mixed = dot("hk,kwc->hwc", tall, times(value_tall, col_coef, 0) * tall_weight[:, None])
    mix_col = to_rows(mixed)

    grad_tall = dot("hk,hwc->kwc", tall, grad_spec)
    grad_row = dot("hk,kwc->hwc", tall, times_conj(grad_tall, col_coef, 0) * tall_weight[:, None])
    grad_value = to_rows(times_conj(grad_row, row_coef, 1))

    col_term = correlate(grad_tall * wide_weight, value_tall, 0, 1, True)
    col_grad = dot("mk,kc->mc", tall, col_term * tall_weight) * scale
    row_term = correlate(grad_row, value_spec, 1, 0, first)
    row_grad = dot("mk,kc->mc", wide_own, row_term * wide_weight) * scale

    gated = (gate_feat * mix_col).astype(bf16)
    grad_gate = grad_out * mix_col
    grad_feat = jnp.concatenate([grad_gate, grad_value], axis=2).astype(bf16)
    grad_framed = jnp.pad(halo(grad_feat), ((0, 0), (1, 1), (0, 0)))
    back_sum = jnp.zeros((tile_rows, width, 2 * channels), f32)
    short_rows = []
    for i in range(3):
        for j in range(3):
            back_sum = back_sum + kernel[i, j] * grad_framed[
                2 - i : 2 - i + tile_rows, 2 - j : 2 - j + width
            ].astype(f32)
            short_rows.append(
                jnp.sum(
                    grad_feat.astype(f32) * framed[i : i + tile_rows, j : j + width].astype(f32),
                    axis=(0, 1),
                )
            )
    back_stack = back_sum.astype(bf16)
    partial_term = dot("rwc,dc->rwd", back_stack, w_both).astype(bf16)
    partial_term = partial_term.reshape(tile_rows, width, lax.axis_size("ch"), channels)
    input_grad = lax.psum_scatter(
        partial_term.reshape(tile_rows, width, -1), "ch", scatter_dimension=2, tiled=True
    )

    weight_term = dot("rwd,rwc->dc", gathered, back_stack) * scale
    short_term = jnp.stack(short_rows).reshape(9, 2 * channels) * scale
    short_term = jnp.concatenate([short_term[:, :channels], short_term[:, channels:]], axis=0)
    depth = weight_term.shape[0]

    def cut(term):
        return term.reshape(tiles, term.shape[0] // tiles, channels)

    packed = jnp.concatenate(
        [
            cut(weight_term[:, :channels]),
            cut(weight_term[:, channels:]),
            cut(row_grad),
            cut(col_grad),
            jnp.broadcast_to(short_term[None], (tiles, 18, channels)),
        ],
        axis=1,
    ).astype(bf16)
    arrived = lax.all_to_all(packed, "grid", split_axis=0, concat_axis=0, tiled=True)
    total = jnp.sum(arrived.astype(f32), axis=0)
    ends = np.cumsum([depth // tiles, depth // tiles, per, height // tiles])
    gate_grad, value_grad, row_share, col_share, short_sum = jnp.split(total, ends, axis=0)
    return (
        gated,
        input_grad,
        gate_grad,
        value_grad,
        short_sum.reshape(2, 3, 3, channels),
        row_share,
        col_share,
    )


def solution(mesh):
    return jax.shard_map(
        local,
        mesh=mesh,
        in_specs=(
            P("grid", None, "ch"),
            P(None, "ch"),
            P(None, "ch"),
            P(None, None, None, "ch"),
            P(None, "ch"),
            P(None, "ch"),
            P("grid", None, "ch"),
        ),
        out_specs=(
            P("grid", None, "ch"),
            P("grid", None, "ch"),
            P("grid", "ch"),
            P("grid", "ch"),
            P(None, None, None, "ch"),
            P("grid", "ch"),
            P("grid", "ch"),
        ),
        check_vma=False,
    )
```

```python
import math

import jax
import jax.numpy as jnp
import ml_dtypes
import numpy as np
from jax import lax
from jax.sharding import PartitionSpec as P

bf16 = jnp.bfloat16
f32 = jnp.float32


def basis(length, tiles):
    half = length // 2
    per = half // tiles
    position = np.arange(length)
    columns, weights = [], []
    for tile in range(tiles):
        freqs = np.arange(tile * per, (tile + 1) * per)
        phase = (position[:, None] * freqs[None, :] % length) * (2.0 * math.pi / length)
        sines = np.sin(phase)
        weight = np.full((2 * per,), 2.0 / length)
        if tile == 0:
            sines[:, 0] = np.where(position % 2 == 0, 1.0, -1.0)
            weight[0] = weight[per] = 1.0 / length
        columns += [np.cos(phase), sines]
        weights.append(weight)
    return np.concatenate(columns, axis=1), np.concatenate(weights)


def parts(spectrum, axis):
    return jnp.split(spectrum, 2, axis=axis)


def filter_parts(spectrum, first):
    cos, sin = parts(spectrum, 0)
    row = lax.broadcasted_iota(jnp.int32, cos.shape, 0) == 0
    packed = jnp.logical_and(row, first)
    return cos, jnp.where(packed, 0.0, sin), jnp.where(packed, sin, cos)


def times(spectrum, coef, axis):
    x, y = parts(spectrum, axis)
    p, q, p2 = coef
    return jnp.concatenate([x * p - y * q, x * q + y * p2], axis=axis)


def times_conj(spectrum, coef, axis):
    x, y = parts(spectrum, axis)
    p, q, p2 = coef
    return jnp.concatenate([x * p + y * q, y * p2 - x * q], axis=axis)


def correlate(a, b, axis, total, first):
    ax, ay = parts(a, axis)
    bx, by = parts(b, axis)
    xx, yy = jnp.sum(ax * bx, axis=total), jnp.sum(ay * by, axis=total)
    cross = jnp.sum(ay * bx - ax * by, axis=total)
    row = lax.broadcasted_iota(jnp.int32, xx.shape, 0) == 0
    packed = jnp.logical_and(row, first)
    return jnp.concatenate(
        [jnp.where(packed, xx, xx + yy), jnp.where(packed, yy, cross)], axis=0
    )


def dot(spec, a, b):
    return jnp.einsum(spec, a.astype(bf16), b.astype(bf16), preferred_element_type=f32)


def neighbours(last, initial):
    size = lax.axis_size("grid")
    before = lax.ppermute(last, "grid", [(i, i + 1) for i in range(size - 1)])
    after = lax.ppermute(initial, "grid", [(i + 1, i) for i in range(size - 1)])
    return before, after


def stencil(rows, kernel, flipped):
    width = rows[0].shape[1]
    framed = jnp.pad(jnp.concatenate(rows, axis=0), ((0, 0), (1, 1), (0, 0)))
    count = len(rows) - 2
    total = jnp.zeros((count, width, rows[0].shape[2]), f32)
    for i in range(3):
        for j in range(3):
            weight = kernel[2 - i, 2 - j] if flipped else kernel[i, j]
            total = total + weight * framed[i : i + count, j : j + width].astype(f32)
    return total.astype(bf16), framed


def split_rows(value):
    return [value[i : i + 1] for i in range(value.shape[0])]


def filter_sums(grad, framed):
    rows, width, _ = grad.shape
    grad = grad.astype(f32)
    return [
        jnp.sum(grad * framed[i : i + rows, j : j + width].astype(f32), axis=(0, 1))
        for i in range(3)
        for j in range(3)
    ]


def scatter_sum(value, mates, others):
    size = lax.axis_size("ch")
    chips = size // 2
    channels = others.shape[1] // chips
    sent = dot("rwc,cd->rwd", value, mates).astype(bf16)
    got = lax.ppermute(sent, "ch", [(i, i ^ 1) for i in range(size)])
    pair = dot("rwc,cd->rwd", value, others) + got.astype(f32)
    total = pair[..., :channels]
    for hop in range(1, chips):
        part = pair[..., hop * channels : (hop + 1) * channels].astype(bf16)
        total = total + lax.ppermute(
            part, "ch", [(i, (i + 2 * hop) % size) for i in range(size)]
        ).astype(f32)
    return total.astype(bf16)


def local(inputs, w_gate, w_value, short_filter, row_filter, column_filter, cotangent):
    tile_rows, width, channels = inputs.shape
    height = column_filter.shape[0]
    tiles = lax.axis_size("grid")
    me = lax.axis_index("grid")
    first = me == 0
    per = width // tiles
    scale = 1.0 / math.sqrt(height * width)
    chips = lax.axis_size("ch") // 2
    spot = lax.axis_index("ch")

    edges = jnp.concatenate([inputs[:1], inputs[-1:]], axis=0)
    edges = lax.all_gather(edges, "ch", axis=2, tiled=True)
    middle = lax.all_gather(inputs[1:-1], "ch", axis=2, tiled=True)
    w_both = jnp.concatenate([w_gate, w_value], axis=1)

    wide, wide_weight = basis(width, tiles)
    tall, tall_weight = basis(height, 1)
    wide = jnp.asarray(wide.astype(ml_dtypes.bfloat16))
    tall = jnp.asarray(tall.astype(ml_dtypes.bfloat16))
    tall_weight = jnp.asarray(tall_weight, f32)[:, None]
    wide_weight = lax.dynamic_slice_in_dim(jnp.asarray(wide_weight, f32), me * per, per, 0)[:, None]
    wide_own = lax.dynamic_slice_in_dim(wide, me * per, per, 1)
    kernel = short_filter.astype(f32)
    row_coef = filter_parts(dot("mk,mc->kc", wide_own, row_filter), first)
    col_coef = filter_parts(dot("mk,mc->kc", tall, column_filter), True)
    col_coef = tuple(v[:, None, :] for v in col_coef)

    def block(hop, swap):
        index = (spot // 2 + hop) % chips * 2 + (spot % 2 + swap) % 2
        return lax.dynamic_slice_in_dim(w_both, index * channels, channels, 0).T

    mates = jnp.concatenate([block(hop, 1) for hop in range(chips)], axis=1)
    others = jnp.concatenate([block(hop, 0) for hop in range(chips)], axis=1)

    edge_proj = dot("rwd,dc->rwc", edges, w_both).astype(bf16)
    edge_b, edge_a = edge_proj[..., channels:], edge_proj[..., :channels]
    before_b, after_b = neighbours(edge_b[1:], edge_b[:1])
    before_a, after_a = neighbours(edge_a[1:], edge_a[:1])
    mid_proj = dot("rwd,dc->rwc", middle, w_both).astype(bf16)
    mid_b, mid_a = mid_proj[..., channels:], mid_proj[..., :channels]
    value_bf, framed_b = stencil(
        [before_b, edge_b[:1], *split_rows(mid_b), edge_b[1:], after_b], kernel[1], False
    )

    def to_columns(field):
        spectrum = dot("wk,rwc->rkc", wide, field).astype(bf16)
        return lax.all_to_all(spectrum, "grid", split_axis=1, concat_axis=0, tiled=True).astype(f32)

    def to_rows(spectrum):
        spectrum = (spectrum * wide_weight).astype(bf16)
        back = lax.all_to_all(spectrum, "grid", split_axis=0, concat_axis=1, tiled=True)
        return dot("wk,rkc->rwc", wide, back)

    value_spec = to_columns(value_bf)
    gate_bf, framed_a = stencil(
        [before_a, edge_a[:1], *split_rows(mid_a), edge_a[1:], after_a], kernel[0], False
    )
    gate_feat = gate_bf.astype(f32)
    grad_out = cotangent.astype(f32)
    grad_mix = (grad_out * gate_feat).astype(bf16)
    grad_spec = to_columns(grad_mix)

    mixed_rows = times(value_spec, row_coef, 1)
    value_tall = dot("hk,hwc->kwc", tall, mixed_rows)
    mixed = dot("hk,kwc->hwc", tall, times(value_tall, col_coef, 0) * tall_weight[:, None])
    mix_col = to_rows(mixed)

    grad_tall = dot("hk,hwc->kwc", tall, grad_spec)
    grad_row = dot("hk,kwc->hwc", tall, times_conj(grad_tall, col_coef, 0) * tall_weight[:, None])
    grad_value = to_rows(times_conj(grad_row, row_coef, 1)).astype(bf16)

    col_term = correlate(grad_tall * wide_weight, value_tall, 0, 1, True)
    col_grad = dot("mk,kc->mc", tall, col_term * tall_weight) * scale
    row_term = correlate(grad_row, value_spec, 1, 0, first)
    row_grad = dot("mk,kc->mc", wide_own, row_term * wide_weight) * scale

    gated = (gate_feat * mix_col).astype(bf16)
    grad_gate = (grad_out * mix_col).astype(bf16)

    def back_parts(grad, filt):
        before, after = neighbours(grad[-1:], grad[:1])
        rows = split_rows(grad)
        middle_back, _ = stencil(rows, filt, True)
        top, _ = stencil([before, rows[0], rows[1]], filt, True)
        bottom, _ = stencil([rows[-2], rows[-1], after], filt, True)
        return middle_back, jnp.concatenate([top, bottom], axis=0)

    mid_back_a, edge_back_a = back_parts(grad_gate, kernel[0])
    mid_back_b, edge_back_b = back_parts(grad_value, kernel[1])
    mid_back = jnp.concatenate([mid_back_a, mid_back_b], axis=2)
    edge_back = jnp.concatenate([edge_back_a, edge_back_b], axis=2)
    mid_grad = scatter_sum(mid_back, mates, others)
    edge_grad = scatter_sum(edge_back, mates, others)
    input_grad = jnp.concatenate([edge_grad[:1], mid_grad, edge_grad[1:]], axis=0)

    gate_term = dot("rwd,rwc->dc", middle, mid_back_a) + dot("rwd,rwc->dc", edges, edge_back_a)
    value_term = dot("rwd,rwc->dc", middle, mid_back_b) + dot("rwd,rwc->dc", edges, edge_back_b)
    short_term = jnp.stack(filter_sums(grad_gate, framed_a) + filter_sums(grad_value, framed_b))
    short_term = short_term * scale
    depth = w_both.shape[0]

    def cut(term):
        return term.reshape(tiles, term.shape[0] // tiles, channels)

    packed = jnp.concatenate(
        [
            cut(gate_term * scale),
            cut(value_term * scale),
            cut(row_grad),
            cut(col_grad),
            jnp.broadcast_to(short_term[None], (tiles, 18, channels)),
        ],
        axis=1,
    ).astype(bf16)
    arrived = lax.all_to_all(packed, "grid", split_axis=0, concat_axis=0, tiled=True)
    total = jnp.sum(arrived.astype(f32), axis=0)
    ends = np.cumsum([depth // tiles, depth // tiles, per, height // tiles])
    gate_grad, value_grad, row_share, col_share, short_sum = jnp.split(total, ends, axis=0)
    return (
        gated,
        input_grad,
        gate_grad,
        value_grad,
        short_sum.reshape(2, 3, 3, channels),
        row_share,
        col_share,
    )


def solution(mesh):
    return jax.shard_map(
        local,
        mesh=mesh,
        in_specs=(
            P("grid", None, "ch"),
            P(None, "ch"),
            P(None, "ch"),
            P(None, None, None, "ch"),
            P(None, "ch"),
            P(None, "ch"),
            P("grid", None, "ch"),
        ),
        out_specs=(
            P("grid", None, "ch"),
            P("grid", None, "ch"),
            P("grid", "ch"),
            P("grid", "ch"),
            P(None, None, None, "ch"),
            P("grid", "ch"),
            P("grid", "ch"),
        ),
        check_vma=False,
    )
```

```python
import math

import jax
import jax.numpy as jnp
import ml_dtypes
import numpy as np
from jax import lax
from jax.sharding import PartitionSpec as P

bf16 = jnp.bfloat16
f32 = jnp.float32


def basis(length, tiles):
    half = length // 2
    per = half // tiles
    position = np.arange(length)
    columns, weights = [], []
    for tile in range(tiles):
        freqs = np.arange(tile * per, (tile + 1) * per)
        phase = (position[:, None] * freqs[None, :] % length) * (2.0 * math.pi / length)
        sines = np.sin(phase)
        weight = np.full((2 * per,), 2.0 / length)
        if tile == 0:
            sines[:, 0] = np.where(position % 2 == 0, 1.0, -1.0)
            weight[0] = weight[per] = 1.0 / length
        columns += [np.cos(phase), sines]
        weights.append(weight)
    return np.concatenate(columns, axis=1), np.concatenate(weights)


def parts(spectrum, axis):
    return jnp.split(spectrum, 2, axis=axis)


def filter_parts(spectrum, first):
    cos, sin = parts(spectrum, 0)
    row = lax.broadcasted_iota(jnp.int32, cos.shape, 0) == 0
    packed = jnp.logical_and(row, first)
    return cos, jnp.where(packed, 0.0, sin), jnp.where(packed, sin, cos)


def times(spectrum, coef, axis):
    x, y = parts(spectrum, axis)
    p, q, p2 = coef
    return jnp.concatenate([x * p - y * q, x * q + y * p2], axis=axis)


def times_conj(spectrum, coef, axis):
    x, y = parts(spectrum, axis)
    p, q, p2 = coef
    return jnp.concatenate([x * p + y * q, y * p2 - x * q], axis=axis)


def correlate(a, b, axis, total, first):
    ax, ay = parts(a, axis)
    bx, by = parts(b, axis)
    xx, yy = jnp.sum(ax * bx, axis=total), jnp.sum(ay * by, axis=total)
    cross = jnp.sum(ay * bx - ax * by, axis=total)
    row = lax.broadcasted_iota(jnp.int32, xx.shape, 0) == 0
    packed = jnp.logical_and(row, first)
    return jnp.concatenate(
        [jnp.where(packed, xx, xx + yy), jnp.where(packed, yy, cross)], axis=0
    )


def dot(spec, a, b):
    return jnp.einsum(spec, a.astype(bf16), b.astype(bf16), preferred_element_type=f32)


def neighbours(last, initial):
    size = lax.axis_size("grid")
    before = lax.ppermute(last, "grid", [(i, i + 1) for i in range(size - 1)])
    after = lax.ppermute(initial, "grid", [(i + 1, i) for i in range(size - 1)])
    return before, after


def stencil(rows, kernel, flipped):
    width = rows[0].shape[1]
    framed = jnp.pad(jnp.concatenate(rows, axis=0), ((0, 0), (1, 1), (0, 0)))
    count = len(rows) - 2
    total = jnp.zeros((count, width, rows[0].shape[2]), f32)
    for i in range(3):
        for j in range(3):
            weight = kernel[2 - i, 2 - j] if flipped else kernel[i, j]
            total = total + weight * framed[i : i + count, j : j + width].astype(f32)
    return total.astype(bf16), framed


def split_rows(value):
    return [value[i : i + 1] for i in range(value.shape[0])]


def filter_sums(grad, framed):
    rows, width, _ = grad.shape
    grad = grad.astype(f32)
    return [
        jnp.sum(grad * framed[i : i + rows, j : j + width].astype(f32), axis=(0, 1))
        for i in range(3)
        for j in range(3)
    ]


def gather(value):
    size = lax.axis_size("ch")
    swap = [(i, i ^ 1) for i in range(size)]
    held = [value] + [
        lax.ppermute(value, "ch", [(i, (i - 2 * hop) % size) for i in range(size)])
        for hop in range(1, size // 2)
    ]
    blocks = []
    for block in held:
        blocks += [block, lax.ppermute(block, "ch", swap)]
    return jnp.concatenate(blocks, axis=2)


def scatter_sum(value, mates, others):
    size = lax.axis_size("ch")
    chips = size // 2
    channels = others.shape[1] // chips
    sent = dot("rwc,cd->rwd", value, mates).astype(bf16)
    got = lax.ppermute(sent, "ch", [(i, i ^ 1) for i in range(size)])
    pair = dot("rwc,cd->rwd", value, others) + got.astype(f32)
    total = pair[..., :channels]
    for hop in range(1, chips):
        part = pair[..., hop * channels : (hop + 1) * channels].astype(bf16)
        total = total + lax.ppermute(
            part, "ch", [(i, (i + 2 * hop) % size) for i in range(size)]
        ).astype(f32)
    return total.astype(bf16)


def local(inputs, w_gate, w_value, short_filter, row_filter, column_filter, cotangent):
    tile_rows, width, channels = inputs.shape
    height = column_filter.shape[0]
    tiles = lax.axis_size("grid")
    me = lax.axis_index("grid")
    first = me == 0
    per = width // tiles
    scale = 1.0 / math.sqrt(height * width)
    chips = lax.axis_size("ch") // 2
    spot = lax.axis_index("ch")

    edges = jnp.concatenate([inputs[:1], inputs[-1:]], axis=0)
    edges = gather(edges)
    middle = gather(inputs[1:-1])
    w_both = jnp.concatenate([w_gate, w_value], axis=1)

    wide, wide_weight = basis(width, tiles)
    tall, tall_weight = basis(height, 1)
    wide = jnp.asarray(wide.astype(ml_dtypes.bfloat16))
    tall = jnp.asarray(tall.astype(ml_dtypes.bfloat16))
    tall_weight = jnp.asarray(tall_weight, f32)[:, None]
    wide_weight = lax.dynamic_slice_in_dim(jnp.asarray(wide_weight, f32), me * per, per, 0)[:, None]
    wide_own = lax.dynamic_slice_in_dim(wide, me * per, per, 1)
    kernel = short_filter.astype(f32)
    row_coef = filter_parts(dot("mk,mc->kc", wide_own, row_filter), first)
    col_coef = filter_parts(dot("mk,mc->kc", tall, column_filter), True)
    col_coef = tuple(v[:, None, :] for v in col_coef)

    def block(hop, swap):
        index = (spot // 2 + hop) % chips * 2 + (spot % 2 + swap) % 2
        return lax.dynamic_slice_in_dim(w_both, index * channels, channels, 0)

    blocks = [[block(hop, swap) for swap in range(2)] for hop in range(chips)]
    mates = jnp.concatenate([pair[1].T for pair in blocks], axis=1)
    others = jnp.concatenate([pair[0].T for pair in blocks], axis=1)
    w_turned = jnp.concatenate([both for pair in blocks for both in pair], axis=0)

    def unturned(term):
        pieces = []
        for chip in range(chips):
            for core in range(2):
                place = (chip - spot // 2) % chips * 2 + (core - spot % 2) % 2
                pieces.append(lax.dynamic_slice_in_dim(term, place * channels, channels, 0))
        return jnp.concatenate(pieces, axis=0)

    edge_proj = dot("rwd,dc->rwc", edges, w_turned).astype(bf16)
    edge_b, edge_a = edge_proj[..., channels:], edge_proj[..., :channels]
    before_b, after_b = neighbours(edge_b[1:], edge_b[:1])
    before_a, after_a = neighbours(edge_a[1:], edge_a[:1])
    mid_proj = dot("rwd,dc->rwc", middle, w_turned).astype(bf16)
    mid_b, mid_a = mid_proj[..., channels:], mid_proj[..., :channels]
    value_bf, framed_b = stencil(
        [before_b, edge_b[:1], *split_rows(mid_b), edge_b[1:], after_b], kernel[1], False
    )

    def spectrum_of(field):
        return dot("wk,rwc->rkc", wide, field).astype(bf16)

    def to_columns(spectrum):
        return lax.all_to_all(spectrum, "grid", split_axis=1, concat_axis=0, tiled=True).astype(f32)

    def to_rows(spectrum):
        spectrum = (spectrum * wide_weight).astype(bf16)
        back = lax.all_to_all(spectrum, "grid", split_axis=0, concat_axis=1, tiled=True)
        return dot("wk,rkc->rwc", wide, back)

    value_rows, before_a, after_a = lax.optimization_barrier(
        (spectrum_of(value_bf), before_a, after_a)
    )
    value_spec = to_columns(value_rows)
    gate_bf, framed_a = stencil(
        [before_a, edge_a[:1], *split_rows(mid_a), edge_a[1:], after_a], kernel[0], False
    )
    gate_feat = gate_bf.astype(f32)
    grad_out = cotangent.astype(f32)
    grad_mix = (grad_out * gate_feat).astype(bf16)
    grad_rows, value_spec = lax.optimization_barrier((spectrum_of(grad_mix), value_spec))
    grad_spec = to_columns(grad_rows)

    mixed_rows = times(value_spec, row_coef, 1)
    value_tall = dot("hk,hwc->kwc", tall, mixed_rows)
    mixed = dot("hk,kwc->hwc", tall, times(value_tall, col_coef, 0) * tall_weight[:, None])
    mix_col = to_rows(mixed)

    grad_tall = dot("hk,hwc->kwc", tall, grad_spec)
    grad_row = dot("hk,kwc->hwc", tall, times_conj(grad_tall, col_coef, 0) * tall_weight[:, None])
    grad_value = to_rows(times_conj(grad_row, row_coef, 1)).astype(bf16)

    col_term = correlate(grad_tall * wide_weight, value_tall, 0, 1, True)
    col_grad = dot("mk,kc->mc", tall, col_term * tall_weight) * scale
    row_term = correlate(grad_row, value_spec, 1, 0, first)
    row_grad = dot("mk,kc->mc", wide_own, row_term * wide_weight) * scale

    gated = (gate_feat * mix_col).astype(bf16)
    grad_gate = (grad_out * mix_col).astype(bf16)

    def back_parts(grad, filt):
        before, after = neighbours(grad[-1:], grad[:1])
        rows = split_rows(grad)
        middle_back, _ = stencil(rows, filt, True)
        top, _ = stencil([before, rows[0], rows[1]], filt, True)
        bottom, _ = stencil([rows[-2], rows[-1], after], filt, True)
        return middle_back, jnp.concatenate([top, bottom], axis=0)

    mid_back_a, edge_back_a = back_parts(grad_gate, kernel[0])
    mid_back_b, edge_back_b = back_parts(grad_value, kernel[1])
    mid_back = jnp.concatenate([mid_back_a, mid_back_b], axis=2)
    edge_back = jnp.concatenate([edge_back_a, edge_back_b], axis=2)
    mid_grad = scatter_sum(mid_back, mates, others)
    edge_grad = scatter_sum(edge_back, mates, others)
    input_grad = jnp.concatenate([edge_grad[:1], mid_grad, edge_grad[1:]], axis=0)

    gate_term = dot("rwd,rwc->dc", middle, mid_back_a) + dot("rwd,rwc->dc", edges, edge_back_a)
    value_term = dot("rwd,rwc->dc", middle, mid_back_b) + dot("rwd,rwc->dc", edges, edge_back_b)
    short_term = jnp.stack(filter_sums(grad_gate, framed_a) + filter_sums(grad_value, framed_b))
    short_term = short_term * scale
    depth = w_both.shape[0]

    def cut(term):
        return term.reshape(tiles, term.shape[0] // tiles, channels)

    packed = jnp.concatenate(
        [
            cut(unturned(gate_term * scale)),
            cut(unturned(value_term * scale)),
            cut(row_grad),
            cut(col_grad),
            jnp.broadcast_to(short_term[None], (tiles, 18, channels)),
        ],
        axis=1,
    ).astype(bf16)
    arrived = lax.all_to_all(packed, "grid", split_axis=0, concat_axis=0, tiled=True)
    total = jnp.sum(arrived.astype(f32), axis=0)
    ends = np.cumsum([depth // tiles, depth // tiles, per, height // tiles])
    gate_grad, value_grad, row_share, col_share, short_sum = jnp.split(total, ends, axis=0)
    return (
        gated,
        input_grad,
        gate_grad,
        value_grad,
        short_sum.reshape(2, 3, 3, channels),
        row_share,
        col_share,
    )


def solution(mesh):
    return jax.shard_map(
        local,
        mesh=mesh,
        in_specs=(
            P("grid", None, "ch"),
            P(None, "ch"),
            P(None, "ch"),
            P(None, None, None, "ch"),
            P(None, "ch"),
            P(None, "ch"),
            P("grid", None, "ch"),
        ),
        out_specs=(
            P("grid", None, "ch"),
            P("grid", None, "ch"),
            P("grid", "ch"),
            P("grid", "ch"),
            P(None, None, None, "ch"),
            P("grid", "ch"),
            P("grid", "ch"),
        ),
        check_vma=False,
    )
```

```python
import math

import jax
import jax.numpy as jnp
import ml_dtypes
import numpy as np
from jax import lax
from jax.sharding import PartitionSpec as P

bf16 = jnp.bfloat16
f32 = jnp.float32


def basis(length, tiles):
    half = length // 2
    per = half // tiles
    position = np.arange(length)
    columns, weights = [], []
    for tile in range(tiles):
        freqs = np.arange(tile * per, (tile + 1) * per)
        phase = (position[:, None] * freqs[None, :] % length) * (2.0 * math.pi / length)
        sines = np.sin(phase)
        weight = np.full((2 * per,), 2.0 / length)
        if tile == 0:
            sines[:, 0] = np.where(position % 2 == 0, 1.0, -1.0)
            weight[0] = weight[per] = 1.0 / length
        columns += [np.cos(phase), sines]
        weights.append(weight)
    return np.concatenate(columns, axis=1), np.concatenate(weights)


def parts(spectrum, axis):
    return jnp.split(spectrum, 2, axis=axis)


def filter_parts(spectrum, first):
    cos, sin = parts(spectrum, 0)
    row = lax.broadcasted_iota(jnp.int32, cos.shape, 0) == 0
    packed = jnp.logical_and(row, first)
    return cos, jnp.where(packed, 0.0, sin), jnp.where(packed, sin, cos)


def times(spectrum, coef, axis):
    x, y = parts(spectrum, axis)
    p, q, p2 = coef
    return jnp.concatenate([x * p - y * q, x * q + y * p2], axis=axis)


def times_conj(spectrum, coef, axis):
    x, y = parts(spectrum, axis)
    p, q, p2 = coef
    return jnp.concatenate([x * p + y * q, y * p2 - x * q], axis=axis)


def correlate(a, b, axis, total, first):
    ax, ay = parts(a, axis)
    bx, by = parts(b, axis)
    xx, yy = jnp.sum(ax * bx, axis=total), jnp.sum(ay * by, axis=total)
    cross = jnp.sum(ay * bx - ax * by, axis=total)
    row = lax.broadcasted_iota(jnp.int32, xx.shape, 0) == 0
    packed = jnp.logical_and(row, first)
    return jnp.concatenate(
        [jnp.where(packed, xx, xx + yy), jnp.where(packed, yy, cross)], axis=0
    )


def dot(spec, a, b):
    return jnp.einsum(spec, a.astype(bf16), b.astype(bf16), preferred_element_type=f32)


def neighbours(last, initial):
    size = lax.axis_size("grid")
    before = lax.ppermute(last, "grid", [(i, i + 1) for i in range(size - 1)])
    after = lax.ppermute(initial, "grid", [(i + 1, i) for i in range(size - 1)])
    return before, after


def stencil(rows, kernel, flipped):
    width = rows[0].shape[1]
    framed = jnp.pad(jnp.concatenate(rows, axis=0), ((0, 0), (1, 1), (0, 0)))
    count = len(rows) - 2
    total = jnp.zeros((count, width, rows[0].shape[2]), f32)
    for i in range(3):
        for j in range(3):
            weight = kernel[2 - i, 2 - j] if flipped else kernel[i, j]
            total = total + weight * framed[i : i + count, j : j + width].astype(f32)
    return total.astype(bf16), framed


def split_rows(value):
    return [value[i : i + 1] for i in range(value.shape[0])]


def filter_sums(grad, framed):
    rows, width, _ = grad.shape
    grad = grad.astype(f32)
    return [
        jnp.sum(grad * framed[i : i + rows, j : j + width].astype(f32), axis=(0, 1))
        for i in range(3)
        for j in range(3)
    ]


def gather(value):
    size = lax.axis_size("ch")
    swap = [(i, i ^ 1) for i in range(size)]
    held = [value] + [
        lax.ppermute(value, "ch", [(i, (i - 2 * hop) % size) for i in range(size)])
        for hop in range(1, size // 2)
    ]
    blocks = []
    for block in held:
        blocks += [block, lax.ppermute(block, "ch", swap)]
    return jnp.concatenate(blocks, axis=2)


def scatter_sum(value, mates, others):
    size = lax.axis_size("ch")
    chips = size // 2
    channels = others.shape[1] // chips
    sent = dot("rwc,cd->rwd", value, mates).astype(bf16)
    got = lax.ppermute(sent, "ch", [(i, i ^ 1) for i in range(size)])
    pair = dot("rwc,cd->rwd", value, others) + got.astype(f32)
    total = pair[..., :channels]
    for hop in range(1, chips):
        part = pair[..., hop * channels : (hop + 1) * channels].astype(bf16)
        total = total + lax.ppermute(
            part, "ch", [(i, (i + 2 * hop) % size) for i in range(size)]
        ).astype(f32)
    return total.astype(bf16)


def local(inputs, w_gate, w_value, short_filter, row_filter, column_filter, cotangent):
    tile_rows, width, channels = inputs.shape
    height = column_filter.shape[0]
    tiles = lax.axis_size("grid")
    me = lax.axis_index("grid")
    first = me == 0
    per = width // tiles
    scale = 1.0 / math.sqrt(height * width)
    chips = lax.axis_size("ch") // 2
    spot = lax.axis_index("ch")

    edges = jnp.concatenate([inputs[:1], inputs[-1:]], axis=0)
    edges = gather(edges)
    middle = gather(inputs[1:-1])
    w_both = jnp.concatenate([w_gate, w_value], axis=1)

    wide, wide_weight = basis(width, tiles)
    tall, tall_weight = basis(height, 1)
    wide = jnp.asarray(wide.astype(ml_dtypes.bfloat16))
    tall = jnp.asarray(tall.astype(ml_dtypes.bfloat16))
    tall_weight = jnp.asarray(tall_weight, f32)[:, None]
    wide_weight = lax.dynamic_slice_in_dim(jnp.asarray(wide_weight, f32), me * per, per, 0)[:, None]
    wide_own = lax.dynamic_slice_in_dim(wide, me * per, per, 1)
    kernel = short_filter.astype(f32)
    row_coef = filter_parts(dot("mk,mc->kc", wide_own, row_filter), first)
    col_coef = filter_parts(dot("mk,mc->kc", tall, column_filter), True)
    col_coef = tuple(v[:, None, :] for v in col_coef)

    def block(hop, swap):
        index = (spot // 2 + hop) % chips * 2 + (spot % 2 + swap) % 2
        return lax.dynamic_slice_in_dim(w_both, index * channels, channels, 0)

    blocks = [[block(hop, swap) for swap in range(2)] for hop in range(chips)]
    mates = jnp.concatenate([pair[1].T for pair in blocks], axis=1)
    others = jnp.concatenate([pair[0].T for pair in blocks], axis=1)
    w_turned = jnp.concatenate([both for pair in blocks for both in pair], axis=0)

    def unturned(term):
        pieces = []
        for chip in range(chips):
            for core in range(2):
                place = (chip - spot // 2) % chips * 2 + (core - spot % 2) % 2
                pieces.append(lax.dynamic_slice_in_dim(term, place * channels, channels, 0))
        return jnp.concatenate(pieces, axis=0)

    edge_proj = dot("rwd,dc->rwc", edges, w_turned).astype(bf16)
    edge_b, edge_a = edge_proj[..., channels:], edge_proj[..., :channels]
    before_b, after_b = neighbours(edge_b[1:], edge_b[:1])
    before_a, after_a = neighbours(edge_a[1:], edge_a[:1])
    mid_proj = dot("rwd,dc->rwc", middle, w_turned).astype(bf16)
    mid_b, mid_a = mid_proj[..., channels:], mid_proj[..., :channels]
    value_bf, framed_b = stencil(
        [before_b, edge_b[:1], *split_rows(mid_b), edge_b[1:], after_b], kernel[1], False
    )

    def spectrum_of(field):
        return dot("wk,rwc->rkc", wide, field).astype(bf16)

    def to_columns(spectrum):
        return lax.all_to_all(spectrum, "grid", split_axis=1, concat_axis=0, tiled=True)

    def to_rows(spectrum):
        return lax.all_to_all(spectrum, "grid", split_axis=0, concat_axis=1, tiled=True)

    def from_spectrum(back):
        return lax.optimization_barrier(dot("wk,rkc->rwc", wide, back).astype(bf16))

    value_rows, before_a, after_a = lax.optimization_barrier(
        (spectrum_of(value_bf), before_a, after_a)
    )
    value_spec = to_columns(value_rows).astype(f32)
    gate_bf, framed_a = stencil(
        [before_a, edge_a[:1], *split_rows(mid_a), edge_a[1:], after_a], kernel[0], False
    )
    gate_feat = gate_bf.astype(f32)
    grad_out = cotangent.astype(f32)
    grad_mix = (grad_out * gate_feat).astype(bf16)
    grad_rows, value_spec = lax.optimization_barrier((spectrum_of(grad_mix), value_spec))
    grad_spec = to_columns(grad_rows)

    mixed_rows = times(value_spec, row_coef, 1)
    value_tall = dot("hk,hwc->kwc", tall, mixed_rows)
    mixed = dot("hk,kwc->hwc", tall, times(value_tall, col_coef, 0) * tall_weight[:, None])
    mixed = (mixed * wide_weight).astype(bf16)
    mixed, grad_spec = lax.optimization_barrier((mixed, grad_spec))
    grad_spec = grad_spec.astype(f32)
    mix_col = from_spectrum(to_rows(mixed)).astype(f32)

    grad_tall = dot("hk,hwc->kwc", tall, grad_spec)
    grad_row = dot("hk,kwc->hwc", tall, times_conj(grad_tall, col_coef, 0) * tall_weight[:, None])
    grad_back = to_rows((times_conj(grad_row, row_coef, 1) * wide_weight).astype(bf16))
    gated = (gate_feat * mix_col).astype(bf16)
    grad_gate = (grad_out * mix_col).astype(bf16)
    gate_halo = neighbours(grad_gate[-1:], grad_gate[:1])
    grad_back, gate_halo = lax.optimization_barrier((grad_back, gate_halo))
    grad_value = from_spectrum(grad_back)
    value_halo = neighbours(grad_value[-1:], grad_value[:1])

    col_term = correlate(grad_tall * wide_weight, value_tall, 0, 1, True)
    col_grad = dot("mk,kc->mc", tall, col_term * tall_weight) * scale
    row_term = correlate(grad_row, value_spec, 1, 0, first)
    row_grad = dot("mk,kc->mc", wide_own, row_term * wide_weight) * scale

    def back_parts(grad, halo, filt):
        before, after = halo
        rows = split_rows(grad)
        middle_back, _ = stencil(rows, filt, True)
        top, _ = stencil([before, rows[0], rows[1]], filt, True)
        bottom, _ = stencil([rows[-2], rows[-1], after], filt, True)
        return middle_back, jnp.concatenate([top, bottom], axis=0)

    mid_back_a, edge_back_a = back_parts(grad_gate, gate_halo, kernel[0])
    mid_back_b, edge_back_b = back_parts(grad_value, value_halo, kernel[1])
    mid_back = jnp.concatenate([mid_back_a, mid_back_b], axis=2)
    edge_back = jnp.concatenate([edge_back_a, edge_back_b], axis=2)
    mid_grad = scatter_sum(mid_back, mates, others)
    edge_grad = scatter_sum(edge_back, mates, others)

    gate_term = dot("rwd,rwc->dc", middle, mid_back_a) + dot("rwd,rwc->dc", edges, edge_back_a)
    value_term = dot("rwd,rwc->dc", middle, mid_back_b) + dot("rwd,rwc->dc", edges, edge_back_b)
    short_term = jnp.stack(filter_sums(grad_gate, framed_a) + filter_sums(grad_value, framed_b))
    short_term = short_term * scale
    depth = w_both.shape[0]

    def cut(term):
        return term.reshape(tiles, term.shape[0] // tiles, channels)

    packed = jnp.concatenate(
        [
            cut(unturned(gate_term * scale)),
            cut(unturned(value_term * scale)),
            cut(row_grad),
            cut(col_grad),
            jnp.broadcast_to(short_term[None], (tiles, 18, channels)),
        ],
        axis=1,
    ).astype(bf16)
    packed, mid_grad = lax.optimization_barrier((packed, mid_grad))
    arrived = lax.all_to_all(packed, "grid", split_axis=0, concat_axis=0, tiled=True)
    input_grad = jnp.concatenate([edge_grad[:1], mid_grad, edge_grad[1:]], axis=0)
    total = jnp.sum(arrived.astype(f32), axis=0)
    ends = np.cumsum([depth // tiles, depth // tiles, per, height // tiles])
    gate_grad, value_grad, row_share, col_share, short_sum = jnp.split(total, ends, axis=0)
    return (
        gated,
        input_grad,
        gate_grad,
        value_grad,
        short_sum.reshape(2, 3, 3, channels),
        row_share,
        col_share,
    )


def solution(mesh):
    return jax.shard_map(
        local,
        mesh=mesh,
        in_specs=(
            P("grid", None, "ch"),
            P(None, "ch"),
            P(None, "ch"),
            P(None, None, None, "ch"),
            P(None, "ch"),
            P(None, "ch"),
            P("grid", None, "ch"),
        ),
        out_specs=(
            P("grid", None, "ch"),
            P("grid", None, "ch"),
            P("grid", "ch"),
            P("grid", "ch"),
            P(None, None, None, "ch"),
            P("grid", "ch"),
            P("grid", "ch"),
        ),
        check_vma=False,
    )
```

```python
import math

import jax
import jax.numpy as jnp
import ml_dtypes
import numpy as np
from jax import lax
from jax.sharding import PartitionSpec as P

bf16 = jnp.bfloat16
f32 = jnp.float32


def basis(length, tiles):
    half = length // 2
    per = half // tiles
    position = np.arange(length)
    columns, weights = [], []
    for tile in range(tiles):
        freqs = np.arange(tile * per, (tile + 1) * per)
        phase = (position[:, None] * freqs[None, :] % length) * (2.0 * math.pi / length)
        sines = np.sin(phase)
        weight = np.full((2 * per,), 2.0 / length)
        if tile == 0:
            sines[:, 0] = np.where(position % 2 == 0, 1.0, -1.0)
            weight[0] = weight[per] = 1.0 / length
        columns += [np.cos(phase), sines]
        weights.append(weight)
    return np.concatenate(columns, axis=1), np.concatenate(weights)


def parts(spectrum, axis):
    return jnp.split(spectrum, 2, axis=axis)


def filter_parts(spectrum, first):
    cos, sin = parts(spectrum, 0)
    row = lax.broadcasted_iota(jnp.int32, cos.shape, 0) == 0
    packed = jnp.logical_and(row, first)
    return cos, jnp.where(packed, 0.0, sin), jnp.where(packed, sin, cos)


def times(spectrum, coef, axis):
    x, y = parts(spectrum, axis)
    p, q, p2 = coef
    return jnp.concatenate([x * p - y * q, x * q + y * p2], axis=axis)


def times_conj(spectrum, coef, axis):
    x, y = parts(spectrum, axis)
    p, q, p2 = coef
    return jnp.concatenate([x * p + y * q, y * p2 - x * q], axis=axis)


def correlate(a, b, axis, total, first):
    ax, ay = parts(a, axis)
    bx, by = parts(b, axis)
    xx, yy = jnp.sum(ax * bx, axis=total), jnp.sum(ay * by, axis=total)
    cross = jnp.sum(ay * bx - ax * by, axis=total)
    row = lax.broadcasted_iota(jnp.int32, xx.shape, 0) == 0
    packed = jnp.logical_and(row, first)
    return jnp.concatenate(
        [jnp.where(packed, xx, xx + yy), jnp.where(packed, yy, cross)], axis=0
    )


def dot(spec, a, b):
    return jnp.einsum(spec, a.astype(bf16), b.astype(bf16), preferred_element_type=f32)


def neighbours(last, initial):
    size = lax.axis_size("grid")
    before = lax.ppermute(last, "grid", [(i, i + 1) for i in range(size - 1)])
    after = lax.ppermute(initial, "grid", [(i + 1, i) for i in range(size - 1)])
    return before, after


def stencil(rows, kernel, flipped):
    width = rows[0].shape[1]
    framed = jnp.pad(jnp.concatenate(rows, axis=0), ((0, 0), (1, 1), (0, 0)))
    count = len(rows) - 2
    total = jnp.zeros((count, width, rows[0].shape[2]), f32)
    for i in range(3):
        for j in range(3):
            weight = kernel[2 - i, 2 - j] if flipped else kernel[i, j]
            total = total + weight * framed[i : i + count, j : j + width].astype(f32)
    return total.astype(bf16), framed


def split_rows(value):
    return [value[i : i + 1] for i in range(value.shape[0])]


def filter_sums(grad, framed):
    rows, width, _ = grad.shape
    grad = grad.astype(f32)
    return [
        jnp.sum(grad * framed[i : i + rows, j : j + width].astype(f32), axis=(0, 1))
        for i in range(3)
        for j in range(3)
    ]


def gather(value):
    size = lax.axis_size("ch")
    swap = [(i, i ^ 1) for i in range(size)]
    held = [value] + [
        lax.ppermute(value, "ch", [(i, (i - 2 * hop) % size) for i in range(size)])
        for hop in range(1, size // 2)
    ]
    blocks = []
    for block in held:
        blocks += [block, lax.ppermute(block, "ch", swap)]
    return jnp.concatenate(blocks, axis=2)


def scatter_start(value, mates, others):
    size = lax.axis_size("ch")
    chips = size // 2
    channels = others.shape[1] // chips
    sent = dot("rwc,cd->rwd", value, mates).astype(bf16)
    got = lax.ppermute(sent, "ch", [(i, i ^ 1) for i in range(size)])
    pair = dot("rwc,cd->rwd", value, others) + got.astype(f32)
    parts_out = [
        pair[..., hop * channels : (hop + 1) * channels].astype(bf16) for hop in range(1, chips)
    ]
    return pair[..., :channels], parts_out


def scatter_end(total, parts_out):
    size = lax.axis_size("ch")
    for hop, part in enumerate(parts_out, 1):
        total = total + lax.ppermute(
            part, "ch", [(i, (i + 2 * hop) % size) for i in range(size)]
        ).astype(f32)
    return total.astype(bf16)


def local(inputs, w_gate, w_value, short_filter, row_filter, column_filter, cotangent):
    tile_rows, width, channels = inputs.shape
    height = column_filter.shape[0]
    tiles = lax.axis_size("grid")
    me = lax.axis_index("grid")
    first = me == 0
    per = width // tiles
    scale = 1.0 / math.sqrt(height * width)
    chips = lax.axis_size("ch") // 2
    spot = lax.axis_index("ch")

    edges = jnp.concatenate([inputs[:1], inputs[-1:]], axis=0)
    edges = gather(edges)
    middle = gather(inputs[1:-1])
    w_both = jnp.concatenate([w_gate, w_value], axis=1)

    wide, wide_weight = basis(width, tiles)
    tall, tall_weight = basis(height, 1)
    wide = jnp.asarray(wide.astype(ml_dtypes.bfloat16))
    tall = jnp.asarray(tall.astype(ml_dtypes.bfloat16))
    tall_weight = jnp.asarray(tall_weight, f32)[:, None]
    wide_weight = lax.dynamic_slice_in_dim(jnp.asarray(wide_weight, f32), me * per, per, 0)[:, None]
    wide_own = lax.dynamic_slice_in_dim(wide, me * per, per, 1)
    kernel = short_filter.astype(f32)
    row_coef = filter_parts(dot("mk,mc->kc", wide_own, row_filter), first)
    col_coef = filter_parts(dot("mk,mc->kc", tall, column_filter), True)
    col_coef = tuple(v[:, None, :] for v in col_coef)

    def block(hop, swap):
        index = (spot // 2 + hop) % chips * 2 + (spot % 2 + swap) % 2
        return lax.dynamic_slice_in_dim(w_both, index * channels, channels, 0)

    blocks = [[block(hop, swap) for swap in range(2)] for hop in range(chips)]
    mates = jnp.concatenate([pair[1].T for pair in blocks], axis=1)
    others = jnp.concatenate([pair[0].T for pair in blocks], axis=1)
    w_turned = jnp.concatenate([both for pair in blocks for both in pair], axis=0)

    def unturned(term):
        pieces = []
        for chip in range(chips):
            for core in range(2):
                place = (chip - spot // 2) % chips * 2 + (core - spot % 2) % 2
                pieces.append(lax.dynamic_slice_in_dim(term, place * channels, channels, 0))
        return jnp.concatenate(pieces, axis=0)

    edge_proj = dot("rwd,dc->rwc", edges, w_turned).astype(bf16)
    edge_b, edge_a = edge_proj[..., channels:], edge_proj[..., :channels]
    before_b, after_b = neighbours(edge_b[1:], edge_b[:1])
    before_a, after_a = neighbours(edge_a[1:], edge_a[:1])
    mid_proj = dot("rwd,dc->rwc", middle, w_turned).astype(bf16)
    mid_b, mid_a = mid_proj[..., channels:], mid_proj[..., :channels]
    value_bf, framed_b = stencil(
        [before_b, edge_b[:1], *split_rows(mid_b), edge_b[1:], after_b], kernel[1], False
    )

    def spectrum_of(field):
        return dot("wk,rwc->rkc", wide, field).astype(bf16)

    def to_columns(spectrum):
        return lax.all_to_all(spectrum, "grid", split_axis=1, concat_axis=0, tiled=True)

    def to_rows(spectrum):
        return lax.all_to_all(spectrum, "grid", split_axis=0, concat_axis=1, tiled=True)

    def from_spectrum(back):
        return lax.optimization_barrier(dot("wk,rkc->rwc", wide, back).astype(bf16))

    value_rows, before_a, after_a = lax.optimization_barrier(
        (spectrum_of(value_bf), before_a, after_a)
    )
    value_spec = to_columns(value_rows).astype(f32)
    gate_bf, framed_a = stencil(
        [before_a, edge_a[:1], *split_rows(mid_a), edge_a[1:], after_a], kernel[0], False
    )
    gate_feat = gate_bf.astype(f32)
    grad_out = cotangent.astype(f32)
    grad_mix = (grad_out * gate_feat).astype(bf16)
    grad_rows, value_spec = lax.optimization_barrier((spectrum_of(grad_mix), value_spec))
    grad_spec = to_columns(grad_rows)

    mixed_rows = times(value_spec, row_coef, 1)
    value_tall = dot("hk,hwc->kwc", tall, mixed_rows)
    mixed = dot("hk,kwc->hwc", tall, times(value_tall, col_coef, 0) * tall_weight[:, None])
    mixed = (mixed * wide_weight).astype(bf16)
    mixed, grad_spec = lax.optimization_barrier((mixed, grad_spec))
    grad_spec = grad_spec.astype(f32)
    mix_col = from_spectrum(to_rows(mixed)).astype(f32)

    grad_tall = dot("hk,hwc->kwc", tall, grad_spec)
    grad_row = dot("hk,kwc->hwc", tall, times_conj(grad_tall, col_coef, 0) * tall_weight[:, None])
    grad_back = to_rows((times_conj(grad_row, row_coef, 1) * wide_weight).astype(bf16))
    gated = (gate_feat * mix_col).astype(bf16)
    grad_gate = (grad_out * mix_col).astype(bf16)
    gate_halo = neighbours(grad_gate[-1:], grad_gate[:1])
    grad_value = from_spectrum(grad_back)
    value_halo = neighbours(grad_value[-1:], grad_value[:1])

    col_term = correlate(grad_tall * wide_weight, value_tall, 0, 1, True)
    col_grad = dot("mk,kc->mc", tall, col_term * tall_weight) * scale
    row_term = correlate(grad_row, value_spec, 1, 0, first)
    row_grad = dot("mk,kc->mc", wide_own, row_term * wide_weight) * scale

    def middle_rows(grad, filt):
        return stencil(split_rows(grad), filt, True)[0]

    def edge_rows(grad, halo, filt):
        before, after = halo
        rows = split_rows(grad)
        top, _ = stencil([before, rows[0], rows[1]], filt, True)
        bottom, _ = stencil([rows[-2], rows[-1], after], filt, True)
        return jnp.concatenate([top, bottom], axis=0)

    mid_back_a = middle_rows(grad_gate, kernel[0])
    mid_back_b = middle_rows(grad_value, kernel[1])
    mid_back = jnp.concatenate([mid_back_a, mid_back_b], axis=2)
    mid_sum, mid_parts = scatter_start(mid_back, mates, others)
    value_halo, mid_parts = lax.optimization_barrier((value_halo, mid_parts))
    mid_grad = scatter_end(mid_sum, mid_parts)

    edge_back_a = edge_rows(grad_gate, gate_halo, kernel[0])
    edge_back_b = edge_rows(grad_value, value_halo, kernel[1])
    edge_back = jnp.concatenate([edge_back_a, edge_back_b], axis=2)
    edge_sum, edge_parts = scatter_start(edge_back, mates, others)
    edge_back_a, edge_back_b, edge_parts = lax.optimization_barrier(
        (edge_back_a, edge_back_b, edge_parts)
    )
    edge_grad = scatter_end(edge_sum, edge_parts)

    gate_term = dot("rwd,rwc->dc", middle, mid_back_a) + dot("rwd,rwc->dc", edges, edge_back_a)
    value_term = dot("rwd,rwc->dc", middle, mid_back_b) + dot("rwd,rwc->dc", edges, edge_back_b)
    short_term = jnp.stack(filter_sums(grad_gate, framed_a) + filter_sums(grad_value, framed_b))
    short_term = short_term * scale
    depth = w_both.shape[0]

    def cut(term):
        return term.reshape(tiles, term.shape[0] // tiles, channels)

    packed = jnp.concatenate(
        [
            cut(unturned(gate_term * scale)),
            cut(unturned(value_term * scale)),
            cut(row_grad),
            cut(col_grad),
            jnp.broadcast_to(short_term[None], (tiles, 18, channels)),
        ],
        axis=1,
    ).astype(bf16)
    packed, mid_grad = lax.optimization_barrier((packed, mid_grad))
    arrived = lax.all_to_all(packed, "grid", split_axis=0, concat_axis=0, tiled=True)
    input_grad = jnp.concatenate([edge_grad[:1], mid_grad, edge_grad[1:]], axis=0)
    total = jnp.sum(arrived.astype(f32), axis=0)
    ends = np.cumsum([depth // tiles, depth // tiles, per, height // tiles])
    gate_grad, value_grad, row_share, col_share, short_sum = jnp.split(total, ends, axis=0)
    return (
        gated,
        input_grad,
        gate_grad,
        value_grad,
        short_sum.reshape(2, 3, 3, channels),
        row_share,
        col_share,
    )


def solution(mesh):
    return jax.shard_map(
        local,
        mesh=mesh,
        in_specs=(
            P("grid", None, "ch"),
            P(None, "ch"),
            P(None, "ch"),
            P(None, None, None, "ch"),
            P(None, "ch"),
            P(None, "ch"),
            P("grid", None, "ch"),
        ),
        out_specs=(
            P("grid", None, "ch"),
            P("grid", None, "ch"),
            P("grid", "ch"),
            P("grid", "ch"),
            P(None, None, None, "ch"),
            P("grid", "ch"),
            P("grid", "ch"),
        ),
        check_vma=False,
    )
```
